32 devices in a mesh: row: 8 (over z, core), col: 4 (over y, x).
Axes of the slice: x: 2, y: 2, z: 4, core: 2. Of those that a mesh axis runs over, the one named last changes fastest.
Arguments:
- loads: float32 [48, 1024, 4096], P(None, 'row', 'col'), may hold values from -6 to 6
- below_first: float32 [47, 1024, 1024], P(None, 'row', 'col'), may hold values from -0.1875 to 0.1875
- below_second: float32 [46, 1024, 1024], P(None, 'row', 'col'), may hold values from -0.1875 to 0.1875
- inverses: float32 [2, 1024, 1024], P(None, None, 'row'), may hold values from -1 to 2, as said below
Outputs:
- solved: float32 [2, 1024, 4096], P(None, None, 'col')
- remaining: float32 [46, 1024, 4096], P(None, 'row', 'col')
The draws below stay inside these ranges and needn't reach their ends.
Inputs may be any that keep to these rules, and one draw needn't show every extreme that they name: `inverses`: each of the two matrices is lower triangular, with a diagonal from 0.5 to 2.
All inputs are finite; a program needn't handle non-finite values.
Results may differ from the reference program's by a relative error of at most 0.000084.
Values sent between devices are 32-bit elements; how exact they have to be, the bound alone decides.
A program may use at most 256 MiB of HBM per device.

```python
import math
import jax
import jax.numpy as jnp
from jax import lax

NB = 1024
CYC = 48
NRHS = 4096


def draw_inverses(key, part):
    key_entries = jax.random.fold_in(key, 11)
    key_diagonal = jax.random.fold_in(key, 12)
    row_index = lax.broadcasted_iota(jnp.int32, (2, NB, NB), 1)
    col_index = lax.broadcasted_iota(jnp.int32, (2, NB, NB), 2)
    entries = jax.random.normal(key_entries, (2, NB, NB), jnp.float32)
    diagonal_vals = jax.random.uniform(key_diagonal, (2, NB, NB), jnp.float32, 0.5, 2.0)
    scaled = entries / math.sqrt(NB)
    triangle = jnp.where(col_index < row_index, scaled, jnp.where(col_index == row_index, diagonal_vals, 0.0))
    return triangle.astype(jnp.float32)


def level_of(rng, dims, pieces, smallest, high):
    loudness, own = 1.0, jax.random.fold_in(rng, 6)
    for axis_at, shards_of in pieces:
        heights = jnp.exp(jax.random.uniform(jax.random.fold_in(own, axis_at), (shards_of,), jnp.float32, smallest / len(pieces), high / len(pieces)))
        loudness = loudness * jnp.repeat(heights, dims[axis_at] // shards_of).reshape([-1 if axis == axis_at else 1 for axis in range(len(dims))])
    return loudness


def bell_draw(rng, dims, scale, limit, split=(), kind=jnp.bfloat16):
    result = jax.random.normal(rng, dims, jnp.float32) * scale
    if len(split) > 0:
        result = level_of(rng, dims, split, -0.22, 0.18) * result
    return jnp.clip(result, min=-limit, max=limit).astype(kind)


def setup_inputs(seed: int = 0) -> dict:
    keys = jax.random.split(jax.random.key(seed), 5)
    return {
        "loads": bell_draw(keys[0], (CYC, NB, NRHS), 1.0, 6.0, ((1, 8), (2, 4)), jnp.float32),
        "below_first": bell_draw(keys[1], (CYC - 1, NB, NB), NB ** -0.5, 0.1875, ((1, 8), (2, 4)), jnp.float32),
        "below_second": bell_draw(keys[2], (CYC - 2, NB, NB), NB ** -0.5, 0.1875, ((1, 8), (2, 4)), jnp.float32),
        "inverses": draw_inverses(jax.random.fold_in(keys[4], 71), 0),
    }


def reference(loads, below_first, below_second, inverses):
    highest = lax.Precision.HIGHEST
    first_block = jnp.dot(inverses[0], loads[0], precision=highest)
    product_one = jnp.dot(below_first.reshape(-1, NB), first_block, precision=highest)
    updated = loads[1:] - product_one.reshape(CYC - 1, NB, NRHS)
    second_block = jnp.dot(inverses[1], updated[0], precision=highest)
    product_two = jnp.dot(below_second.reshape(-1, NB), second_block, precision=highest)
    remaining = updated[1:] - product_two.reshape(CYC - 2, NB, NRHS)
    return jnp.stack([first_block, second_block]), remaining
```

```python
import functools
import jax
import jax.numpy as jnp
from jax import lax
from jax.experimental import pallas as pl
from jax.experimental.pallas import tpu as pltpu
from jax.sharding import PartitionSpec as P

HIGH = lax.Precision.HIGH
STEP = 4


def chunk_sizes(count):
    tail = count % STEP
    steps = count // STEP
    sizes = []
    for share in (4, 3, 3):
        now = min(-(-steps * share // 11), steps - sum(sizes))
        if now > 0:
            sizes.append(now)
    if steps > sum(sizes):
        sizes.append(steps - sum(sizes))
    return [size * STEP for size in sizes] + ([tail] if tail else [])


def halves(value):
    high = lax.reduce_precision(value, 8, 7)
    return high.astype(jnp.bfloat16), (value - high).astype(jnp.bfloat16)


def update_kernel(step, a1, a2, *refs):
    loads = refs[:step // 2]
    f1h, f1l, f2h, f2l = refs[step // 2:step // 2 + 4]
    out = refs[-1]
    rows = a1.shape[1]
    total = None
    for a, fh, fl in ((a1, f1h, f1l), (a2, f2h, f2l)):
        whole = a[...].reshape(step * rows, a.shape[2])
        high = whole.astype(jnp.bfloat16)
        low = (whole - high.astype(jnp.float32)).astype(jnp.bfloat16)
        for x, y in ((high, fh), (high, fl), (low, fh)):
            term = jnp.dot(x, y[...], preferred_element_type=jnp.float32)
            total = term if total is None else total + term
    total = total.reshape(step, rows, total.shape[1])
    for at, part in enumerate(loads):
        out[2 * at:2 * at + 2] = part[...] - total[2 * at:2 * at + 2]


def update_chunk(a1, a2, loads, factors, offset, previous):
    size, rows, depth = a1.shape
    columns = loads.shape[2]
    count = loads.shape[0] - 2
    step = STEP if size % STEP == 0 else 2
    pairs = step // 2
    block = pl.BlockSpec((step, rows, depth), lambda i: (i, 0, 0))
    load_specs = [
        pl.BlockSpec((2, rows, columns), lambda i, k=k: (1 + offset // 2 + i * pairs + k, 0, 0))
        for k in range(pairs)
    ]
    full = pl.BlockSpec((depth, columns), lambda i: (0, 0), pipeline_mode=pl.Buffered(1))
    operands = [a1, a2] + [loads] * pairs + list(factors)
    in_specs = [block, block] + load_specs + [full] * 4
    aliases = {}
    if previous is not None:
        aliases = {len(operands): 0}
        operands.append(previous)
        in_specs.append(pl.BlockSpec(memory_space=pl.ANY))
    work = size * rows * depth * columns
    return pl.pallas_call(
        functools.partial(update_kernel, step),
        out_shape=jax.ShapeDtypeStruct((count, rows, columns), jnp.float32),
        grid=(size // step,),
        in_specs=in_specs,
        out_specs=pl.BlockSpec((step, rows, columns), lambda i: (offset // step + i, 0, 0)),
        input_output_aliases=aliases,
        compiler_params=pltpu.CompilerParams(vmem_limit_bytes=48 * 1024 * 1024),
        cost_estimate=pl.CostEstimate(
            flops=12 * work,
            bytes_accessed=8 * size * rows * (depth + columns) + 8 * depth * columns,
            transcendentals=0,
        ),
    )(*operands)


def local(loads, below_first, below_second, inverses):
    cycles = loads.shape[0]
    gather = lambda piece: lax.all_gather(piece, "col", axis=2, tiled=True)
    slices = []
    at = 0
    for size in chunk_sizes(cycles - 2):
        slices.append([below_first[at + 1:at + 1 + size], below_second[at:at + size], at])
        at += size
    top = gather(below_first[:1])
    early = [gather(piece) for piece in slices[0][:2]]
    first_block = lax.psum(jnp.dot(inverses[0], loads[0], precision=HIGH), "row")
    later = [piece[:2] for piece in slices[1:]]
    first_block, later = lax.optimization_barrier((first_block, later))
    updated = loads[1] - jnp.dot(top[0], first_block, precision=HIGH)
    updated, early = lax.optimization_barrier((updated, early))
    second_block = lax.psum(jnp.dot(inverses[1], updated, precision=HIGH), "row")
    factors = halves(first_block) + halves(second_block)
    pieces = [early] + [[gather(piece) for piece in pair] for pair in later]
    remaining = None
    for (a1, a2), (_, _, offset) in zip(pieces, slices):
        remaining = update_chunk(a1, a2, loads, factors, offset, remaining)
    return (jnp.stack([first_block, second_block]), remaining)


def solution(mesh):
    in_specs = (
        P(None, "row", "col"),
        P(None, "row", "col"),
        P(None, "row", "col"),
        P(None, None, "row"),
    )
    out_specs = (P(None, None, "col"), P(None, "row", "col"))
    return jax.shard_map(local, mesh=mesh, in_specs=in_specs, out_specs=out_specs, check_vma=False)
```

```python
import functools
import jax
import jax.numpy as jnp
from jax import lax
from jax.experimental import pallas as pl
from jax.experimental.pallas import tpu as pltpu
from jax.sharding import PartitionSpec as P

HIGH = lax.Precision.HIGH
STEP = 4


def chunk_sizes(count):
    last = 4
    middle = count * 2 // 5 // 2 * 2
    return [count - middle - last, middle, last]


def halves(value):
    high = lax.reduce_precision(value, 8, 7)
    return high.astype(jnp.bfloat16), (value - high).astype(jnp.bfloat16)


def update_kernel(step, a1, a2, *refs):
    loads = refs[:step // 2]
    f1h, f1l, f2h, f2l = refs[step // 2:step // 2 + 4]
    out = refs[-1]
    rows = a1.shape[1]
    total = None
    for a, fh, fl in ((a1, f1h, f1l), (a2, f2h, f2l)):
        whole = a[...].reshape(step * rows, a.shape[2])
        high = whole.astype(jnp.bfloat16)
        low = (whole - high.astype(jnp.float32)).astype(jnp.bfloat16)
        for x, y in ((high, fh), (high, fl), (low, fh)):
            term = jnp.dot(x, y[...], preferred_element_type=jnp.float32)
            total = term if total is None else total + term
    total = total.reshape(step, rows, total.shape[1])
    for at, part in enumerate(loads):
        out[2 * at:2 * at + 2] = part[...] - total[2 * at:2 * at + 2]


def update_chunk(both, loads, factors, offset, previous):
    rows, depth = both.shape[1:]
    size = both.shape[0] // 2
    columns = loads.shape[2]
    count = loads.shape[0] - 2
    step = STEP if size % STEP == 0 and offset % STEP == 0 else 2
    pairs = step // 2
    block = pl.BlockSpec((step, rows, depth), lambda i: (i, 0, 0))
    block2 = pl.BlockSpec((step, rows, depth), lambda i: (size // step + i, 0, 0))
    load_specs = [
        pl.BlockSpec((2, rows, columns), lambda i, k=k: (1 + offset // 2 + i * pairs + k, 0, 0))
        for k in range(pairs)
    ]
    full = pl.BlockSpec((depth, columns), lambda i: (0, 0), pipeline_mode=pl.Buffered(1))
    operands = [both, both] + [loads] * pairs + list(factors)
    in_specs = [block, block2] + load_specs + [full] * 4
    aliases = {}
    if previous is not None:
        aliases = {len(operands): 0}
        operands.append(previous)
        in_specs.append(pl.BlockSpec(memory_space=pl.ANY))
    work = size * rows * depth * columns
    return pl.pallas_call(
        functools.partial(update_kernel, step),
        out_shape=jax.ShapeDtypeStruct((count, rows, columns), jnp.float32),
        grid=(size // step,),
        in_specs=in_specs,
        out_specs=pl.BlockSpec((step, rows, columns), lambda i: (offset // step + i, 0, 0)),
        input_output_aliases=aliases,
        compiler_params=pltpu.CompilerParams(vmem_limit_bytes=48 * 1024 * 1024),
        cost_estimate=pl.CostEstimate(
            flops=12 * work,
            bytes_accessed=8 * size * rows * (depth + columns) + 8 * depth * columns,
            transcendentals=0,
        ),
    )(*operands)


def local(loads, below_first, below_second, inverses):
    cycles = loads.shape[0]
    gather = lambda piece: lax.all_gather(piece, "col", axis=2, tiled=True)
    chunks, offsets = [], []
    at = 0
    for size in chunk_sizes(cycles - 2):
        chunks.append(jnp.concatenate([below_first[at + 1:at + 1 + size], below_second[at:at + size]]))
        offsets.append(at)
        at += size
    inverses, chunks[0] = lax.optimization_barrier((inverses, chunks[0]))
    early = gather(chunks[0])
    top = gather(below_first[:1])
    first_block = lax.psum(jnp.dot(inverses[0], loads[0], precision=HIGH), "row")
    first_block, later = lax.optimization_barrier((first_block, chunks[1:]))
    updated = loads[1] - jnp.dot(top[0], first_block, precision=HIGH)
    terms = jnp.dot(inverses[1], updated, precision=HIGH)
    terms, early = lax.optimization_barrier((terms, early))
    second_block = lax.psum(terms, "row")
    factors = halves(first_block) + halves(second_block)
    remaining = None
    for both, offset in zip([early] + [gather(chunk) for chunk in later], offsets):
        remaining = update_chunk(both, loads, factors, offset, remaining)
    return (jnp.stack([first_block, second_block]), remaining)


def solution(mesh):
    in_specs = (
        P(None, "row", "col"),
        P(None, "row", "col"),
        P(None, "row", "col"),
        P(None, None, "row"),
    )
    out_specs = (P(None, None, "col"), P(None, "row", "col"))
    return jax.shard_map(local, mesh=mesh, in_specs=in_specs, out_specs=out_specs, check_vma=False)
```
